32 devices in a mesh: node: 8 (over z, core), local: 4 (over y, x).
Axes of the slice: x: 2, y: 2, z: 4, core: 2. Of those that a mesh axis runs over, the one named last changes fastest.
Arguments:
- grad_out: bfloat16 [512, 4096], P(('node', 'local')), may hold values from -6 to 6
- gate_pre: bfloat16 [512, 14592], P('node', 'local'), may hold values from -6 to 6
- up_pre: bfloat16 [512, 14592], P('node', 'local'), may hold values from -6 to 6
- w_down: bfloat16 [14592, 4096], P('local'), may hold values from -0.046875 to 0.046875
Outputs:
- grad_gate: bfloat16 [512, 14592], P('node', 'local')
- grad_up: bfloat16 [512, 14592], P('node', 'local')
- grad_weight: float32 [14592, 4096], P(('local', 'node'))
The draws below stay inside these ranges and needn't reach their ends.
All inputs are finite; a program needn't handle non-finite values.
Results may differ from the reference program's by a relative error of at most 0.0029.
Values may be sent and summed in bfloat16 or wider, within the bound.
A program may use at most 192 MiB of HBM per device.

```python
import jax
import jax.numpy as jnp

D = 4096
FFW = 14592
TOKENS = 512


def strengthened(array, key, source, target, blocks, factor):
    def block_of(position):
        return (jnp.arange(array.shape[position]) // (array.shape[position] // blocks)).reshape((-1,) + (1,) * (array.ndim - 1 - position))

    one_side = jax.random.permutation(key, blocks)[block_of(target)]
    second = (block_of(target) + blocks // 2) % blocks
    return jnp.where((block_of(source) == one_side) | (block_of(source) == second), factor * array, array)


def shard_levels(key, shape, shards, least, top_value):
    gain, own = 1.0, jax.random.fold_in(key, 6)
    for dim, shards_of in shards:
        heights = jnp.exp(jax.random.uniform(jax.random.fold_in(own, dim), (shards_of,), jnp.float32, least / len(shards), top_value / len(shards)))
        gain = gain * jnp.repeat(heights, shape[dim] // shards_of).reshape([-1 if axis == dim else 1 for axis in range(len(shape))])
    return gain


def scatter_about(key, extent, deviation, limit, split=(), held_as=jnp.bfloat16):
    gain = shard_levels(key, extent, split, -0.22, 0.18) if split else 1.0
    values = jax.random.normal(key, extent, jnp.float32) * deviation * gain
    return jnp.minimum(jnp.maximum(values, -limit), limit).astype(held_as)


def noise_with(stream_key, extent, width, limit, cuts, heavy, held_as=jnp.bfloat16):
    result = width * jax.random.normal(stream_key, extent, jnp.float32)
    if cuts:
        result = result * shard_levels(stream_key, extent, cuts, -0.22, 0.18)
    return jnp.clip(strengthened(result, jax.random.fold_in(stream_key, 3), *heavy), -limit, limit).astype(held_as)


def setup_inputs(seed: int = 0) -> dict:
    arg_keys = jax.random.split(jax.random.key(seed), 5)
    grad_out = scatter_about(arg_keys[0], (TOKENS, D), 1.0, 6.0, ((0, 32),))
    gate_pre = scatter_about(arg_keys[1], (TOKENS, FFW), 1.5, 6.0, ((0, 8), (1, 4)))
    up_pre = noise_with(arg_keys[2], (TOKENS, FFW), 1.0, 6.0, ((0, 8), (1, 4)), (0, 1, 8, 2.0))
    w_down = scatter_about(arg_keys[3], (FFW, D), FFW ** -0.5, 0.046875, ((0, 4),))
    return dict(grad_out=grad_out, gate_pre=gate_pre, up_pre=up_pre, w_down=w_down)


def reference(grad_out, gate_pre, up_pre, w_down):
    gate = gate_pre.astype(jnp.float32)
    up = up_pre.astype(jnp.float32)
    sig = jax.nn.sigmoid(gate)
    act = gate * sig
    hidden = (act * up).astype(jnp.bfloat16)
    grad_hidden = jnp.dot(grad_out, w_down.T, preferred_element_type=jnp.float32)
    grad_up = (grad_hidden * act).astype(jnp.bfloat16)
    grad_gate = (grad_hidden * up * sig * (1.0 + gate * (1.0 - sig))).astype(jnp.bfloat16)
    grad_weight = jnp.dot(hidden.T, grad_out, preferred_element_type=jnp.float32)
    return grad_gate, grad_up, grad_weight
```

```python
import jax
import jax.numpy as jnp
from jax import lax
from jax.sharding import PartitionSpec as P


def factors(gate_pre, up_pre):
    gate = gate_pre.astype(jnp.float32)
    up = up_pre.astype(jnp.float32)
    sig = jax.nn.sigmoid(gate)
    return gate, up, sig, gate * sig


def summed(grad_out, gate_pre, up_pre, w_down):
    gate, up, sig, act = factors(gate_pre, up_pre)
    hidden = (act * up).astype(jnp.bfloat16)
    node_grad = lax.all_gather(grad_out, "local", axis=0, tiled=True)
    grad_hidden = jnp.einsum("td,fd->tf", node_grad, w_down, preferred_element_type=jnp.float32)
    grad_up = (grad_hidden * act).astype(jnp.bfloat16)
    grad_gate = (grad_hidden * up * sig * (1.0 + gate * (1.0 - sig))).astype(jnp.bfloat16)
    partial_value = jnp.einsum("tf,td->fd", hidden, node_grad, preferred_element_type=jnp.float32)
    grad_weight = lax.psum_scatter(partial_value, "node", scatter_dimension=0, tiled=True)
    return (grad_gate, grad_up, grad_weight)


def gathered(grad_out, gate_pre, up_pre, w_down):
    gate, up, sig, act = factors(gate_pre, up_pre)
    hidden = (act * up).astype(jnp.bfloat16)
    mine = lax.all_to_all(hidden, "node", split_axis=1, concat_axis=0, tiled=True)
    all_grad = lax.all_gather(grad_out, ("node", "local"), axis=0, tiled=True)
    tokens = gate_pre.shape[0]
    node_grad = lax.dynamic_slice_in_dim(all_grad, lax.axis_index("node") * tokens, tokens, 0)
    grad_hidden = jnp.einsum("td,fd->tf", node_grad, w_down, preferred_element_type=jnp.float32)
    grad_up = (grad_hidden * act).astype(jnp.bfloat16)
    grad_gate = (grad_hidden * up * sig * (1.0 + gate * (1.0 - sig))).astype(jnp.bfloat16)
    grad_weight = jnp.einsum("tf,td->fd", mine, all_grad, preferred_element_type=jnp.float32)
    return (grad_gate, grad_up, grad_weight)


def solution(mesh):
    devices = mesh.shape["node"] * mesh.shape["local"]

    def on_device(grad_out, gate_pre, up_pre, w_down):
        gather_bytes = devices * grad_out.size * 2
        sum_bytes = w_down.size * 4
        plan = gathered if gather_bytes < sum_bytes else summed
        return plan(grad_out, gate_pre, up_pre, w_down)

    return jax.shard_map(
        on_device,
        mesh=mesh,
        in_specs=(
            P(("node", "local"), None),
            P("node", "local"),
            P("node", "local"),
            P("local", None),
        ),
        out_specs=(P("node", "local"), P("node", "local"), P(("local", "node"), None)),
        check_vma=False,
    )
```

```python
import functools

import jax
import jax.numpy as jnp
from jax import lax
from jax.experimental import pallas as pl
from jax.experimental.pallas import tpu as pltpu
from jax.sharding import PartitionSpec as P

MESH = pl.DeviceIdType.MESH
LANES = 128
STEP = 384


def factors(gate_pre, up_pre):
    gate = gate_pre.astype(jnp.float32)
    up = up_pre.astype(jnp.float32)
    sig = jax.nn.sigmoid(gate)
    return gate, up, sig, gate * sig


def summed(grad_out, gate_pre, up_pre, w_down):
    gate, up, sig, act = factors(gate_pre, up_pre)
    hidden = (act * up).astype(jnp.bfloat16)
    node_grad = lax.all_gather(grad_out, "local", axis=0, tiled=True)
    grad_hidden = jnp.einsum("td,fd->tf", node_grad, w_down, preferred_element_type=jnp.float32)
    grad_up = (grad_hidden * act).astype(jnp.bfloat16)
    grad_gate = (grad_hidden * up * sig * (1.0 + gate * (1.0 - sig))).astype(jnp.bfloat16)
    partial_value = jnp.einsum("tf,td->fd", hidden, node_grad, preferred_element_type=jnp.float32)
    grad_weight = lax.psum_scatter(partial_value, "node", scatter_dimension=0, tiled=True)
    return (grad_gate, grad_up, grad_weight)


def exchange(nodes, go, gate, up, w, all_grad, all_hidden, gg, gu,
             wv, ng, hf, hs, xs, xr, ys, yr, xhs, xhr, yhs, yhr, zs, zr, ss, sr, hss, hsr, ws, ls):
    n, l = lax.axis_index("node"), lax.axis_index("local")
    levels = nodes // 2
    z, c = lax.div(n, 2), lax.rem(n, 2)
    y, x = lax.div(l, 2), lax.rem(l, 2)
    lx, ly, ld = y * 2 + 1 - x, (1 - y) * 2 + x, (1 - y) * 2 + 1 - x
    xn, yn, sib = (n, lx), (n, ly), (z * 2 + 1 - c, l)
    rows, width = go.shape
    half = width // 2
    tokens, hidden_units = gate.shape
    block = hidden_units // nodes
    padded = hs.shape[2]

    starts = list(range(0, hidden_units, STEP))
    full = hidden_units // STEP

    def w_copy(i, size=STEP):
        at = pl.ds(i * STEP if isinstance(i, int) else pl.multiple_of(i * STEP, STEP), size)
        return pltpu.make_async_copy(w.at[at, :], wv.at[at, :], ws.at[i])

    for i, start in enumerate(starts):
        w_copy(i, min(STEP, hidden_units - start)).start()

    barrier = pltpu.get_barrier_semaphore()
    for peer in [xn, yn] + [(lax.rem(n + k, nodes), l) for k in range(1, nodes)]:
        pl.semaphore_signal(barrier, inc=1, device_id=peer, device_id_type=MESH)
    pl.semaphore_wait(barrier, nodes + 1)

    def slot(level, core, local, part=None):
        at = pl.ds(pl.multiple_of(((level * 2 + core) * 4 + local) * rows, rows), rows)
        if part is None:
            return all_grad.at[at, :]
        return all_grad.at[at, pl.ds(part * half, half)]

    def remote(source, target, sent, received, device):
        return pltpu.make_async_remote_copy(
            src_ref=source, dst_ref=target, send_sem=sent, recv_sem=received,
            device_id=device, device_id_type=MESH)

    def arrived(target, received):
        remote(target, target, hss.at[0], received, xn).wait_recv()

    start, sent = (lambda copy: copy.start()), (lambda copy: copy.wait_send())

    def along(level, source, side, act):
        can = z > 0 if side < 0 else z < levels - 1
        to = (n + 2 * side, l)

        @pl.when(can)
        def _():
            act(remote(source, slot(level, c, l), zs.at[(side + 1) // 2, level], zr.at[level], to))

    def across(level, source, act):
        target = slot(level, c, l)
        act(remote(source, target, xs.at[level], xr.at[level], xn))
        act(remote(source, target, ys.at[level], yr.at[level], yn))
        act(remote(source, target, ss.at[level, l], sr.at[level, l], sib))

    def from_x(level, act):
        part, whole = slot(level, c, lx, 0), slot(level, c, lx)
        act(remote(part, part, yhs.at[level], yhr.at[level], yn))
        act(remote(whole, whole, ss.at[level, lx], sr.at[level, lx], sib))

    def from_y(level, act):
        part, whole = slot(level, c, ly, 1), slot(level, c, ly)
        act(remote(part, part, xhs.at[level], xhr.at[level], xn))
        act(remote(whole, whole, ss.at[level, ly], sr.at[level, ly], sib))

    def from_d(level, act):
        whole = slot(level, c, ld)
        act(remote(whole, whole, ss.at[level, ld], sr.at[level, ld], sib))

    def each(distance, run):
        for side in (-1, 1):
            level = z + side * distance

            @pl.when((level >= 0) & (level < levels))
            def _():
                run(level, side)

    def z_event(level, side):
        arrived(slot(level, c, l), zr.at[level])
        source = slot(level, c, l)
        along(level, source, -side, start)
        across(level, source, start)

    def xy_event(level, side=0):
        arrived(slot(level, c, lx), xr.at[level])
        from_x(level, start)
        arrived(slot(level, c, ly), yr.at[level])
        from_y(level, start)

    def d_event(level, side=0):
        arrived(slot(level, c, ld, 0), yhr.at[level])
        arrived(slot(level, c, ld, 1), xhr.at[level])
        from_d(level, start)

    for side in (-1, 1):
        along(z, go, side, start)
    across(z, go, start)
    own = pltpu.make_async_copy(go, slot(z, c, l), ls.at[0])
    own.start()

    spread = hf.shape[1]
    last = hidden_units // LANES * LANES
    if spread > last:
        hf[:, last:] = jnp.zeros((tokens, spread - last), jnp.float32)

    @pl.loop(0, tokens // 16)
    def _(i):
        at = pl.ds(pl.multiple_of(i * 16, 16), 16)
        for first in range(0, hidden_units, 512):
            columns = slice(first, min(first + 512, hidden_units))
            g = gate[at, columns].astype(jnp.float32)
            hf[at, columns] = g * jax.nn.sigmoid(g) * up[at, columns].astype(jnp.float32)

    @pl.loop(0, tokens // 16)
    def _(i):
        at = pl.ds(pl.multiple_of(i * 16, 16), 16)
        for k in range(nodes):
            base = k * block // LANES * LANES
            shift = k * block - base
            window = padded + (LANES if shift else 0)
            values = hf[at, base:base + window]
            if shift:
                values = pltpu.roll(values, window - shift, 1)[:, :padded]
            hs[k, at, :] = values.astype(jnp.bfloat16)

    def hidden_copy(k):
        to = lax.rem(n + k, nodes)
        return remote(hs.at[to], all_hidden.at[n], hss.at[k], hsr.at[n], (to, l))

    for k in range(1, nodes):
        hidden_copy(k).start()
    own_hidden = pltpu.make_async_copy(hs.at[n], all_hidden.at[n], ls.at[1])
    own_hidden.start()

    def multiply(i, size=STEP):
        w_copy(i, size).wait()
        at = pl.ds(i * STEP if isinstance(i, int) else pl.multiple_of(i * STEP, STEP), size)
        grad = lax.dot_general(ng[...], wv[at, :], (((1,), (1,)), ((), ())),
                               preferred_element_type=jnp.float32)
        g, u = gate[:, at].astype(jnp.float32), up[:, at].astype(jnp.float32)
        sig = jax.nn.sigmoid(g)
        gu[:, at] = (grad * (g * sig)).astype(jnp.bfloat16)
        gg[:, at] = (grad * u * sig * (1.0 + g * (1.0 - sig))).astype(jnp.bfloat16)

    def multiply_some(part, parts):
        first, stop = full * part // parts, full * (part + 1) // parts

        @pl.loop(first, stop)
        def _(i):
            multiply(i)

    xy_event(z)
    if levels > 1:
        each(1, z_event)
    d_event(z)
    own.wait()
    node_rows = pl.ds(pl.multiple_of(n * tokens, tokens), tokens)
    load = pltpu.make_async_copy(all_grad.at[node_rows, :], ng, ls.at[2])
    load.start()
    load.wait()
    parts = 2 * levels - 1
    for distance in range(1, levels):
        multiply_some(2 * distance - 2, parts)
        if distance + 1 < levels:
            each(distance + 1, z_event)
        each(distance, xy_event)
        multiply_some(2 * distance - 1, parts)
        each(distance, d_event)
    multiply_some(parts - 1, parts)
    if hidden_units % STEP:
        multiply(full, hidden_units % STEP)

    @pl.loop(0, levels)
    def _(level):
        for local in range(4):
            arrived(slot(level, 1 - c, local), sr.at[level, local])

    for k in range(1, nodes):
        other = lax.rem(n + k, nodes)
        arrived(all_hidden.at[other], hsr.at[other])
        hidden_copy(k).wait_send()
    own_hidden.wait()

    def z_sent(level, side):
        along(level, slot(level, c, l), -side, sent)

    for side in (-1, 1):
        along(z, go, side, sent)
    for distance in range(1, levels):
        each(distance, z_sent)

    @pl.loop(0, levels)
    def _(level):
        across(level, slot(level, c, l), sent)
        from_x(level, sent)
        from_y(level, sent)
        from_d(level, sent)


def weight(hidden, grads, gg, gu, out, gg_out, gu_out, turned, sems):
    copies = [pltpu.make_async_copy(gg, gg_out, sems.at[0]), pltpu.make_async_copy(gu, gu_out, sems.at[1])]
    i = pl.program_id(0)

    @pl.when(i == 0)
    def _():
        for copy in copies:
            copy.start()
        turned[...] = hidden[...].T

    rows = out.shape[0]
    out[...] = jnp.dot(turned[...], grads[...], preferred_element_type=jnp.float32)[:rows]

    @pl.when(i == pl.num_programs(0) - 1)
    def _():
        for copy in copies:
            copy.wait()


def gathered(nodes, grad_out, gate_pre, up_pre, w_down):
    tokens, hidden_units = gate_pre.shape
    rows, width = grad_out.shape
    levels = nodes // 2
    block = hidden_units // nodes
    padded = -(-block // LANES) * LANES
    spread = max(k * block // LANES * LANES + padded + LANES for k in range(nodes))
    everyone = nodes * 4 * rows
    chunks = -(-hidden_units // STEP)
    vmem, hbm = pl.BlockSpec(memory_space=pltpu.VMEM), pl.BlockSpec(memory_space=pl.ANY)
    dma = pltpu.SemaphoreType.DMA
    bf16 = jnp.bfloat16
    all_grad, all_hidden, gg, gu = pl.pallas_call(
        functools.partial(exchange, nodes),
        out_shape=(
            jax.ShapeDtypeStruct((everyone, width), bf16),
            jax.ShapeDtypeStruct((nodes, tokens, padded), bf16),
            jax.ShapeDtypeStruct(gate_pre.shape, bf16),
            jax.ShapeDtypeStruct(gate_pre.shape, bf16),
        ),
        in_specs=[vmem, vmem, vmem, hbm],
        out_specs=(hbm, hbm, vmem, vmem),
        scratch_shapes=[
            pltpu.VMEM(w_down.shape, bf16),
            pltpu.VMEM((tokens, width), bf16),
            pltpu.VMEM((tokens, spread), jnp.float32),
            pltpu.VMEM((nodes, tokens, padded), bf16),
        ] + [dma((levels,))] * 8 + [
            dma((2, levels)), dma((levels,)),
            dma((levels, 4)), dma((levels, 4)),
            dma((nodes,)), dma((nodes,)),
            dma((chunks,)), dma((3,)),
        ],
        compiler_params=pltpu.CompilerParams(
            collective_id=0, has_side_effects=True, vmem_limit_bytes=56 * 1024 * 1024),
        cost_estimate=pl.CostEstimate(
            flops=2 * tokens * hidden_units * width, transcendentals=2 * tokens * hidden_units,
            bytes_accessed=2 * w_down.size),
        name="exchange",
    )(grad_out, gate_pre, up_pre, w_down)

    columns = 512
    grad_weight, gg, gu = pl.pallas_call(
        weight,
        grid=(width // columns,),
        out_shape=(
            jax.ShapeDtypeStruct((block, width), jnp.float32),
            jax.ShapeDtypeStruct(gate_pre.shape, bf16),
            jax.ShapeDtypeStruct(gate_pre.shape, bf16),
        ),
        in_specs=[
            pl.BlockSpec((everyone // 4 // rows * tokens, padded), lambda i: (0, 0)),
            pl.BlockSpec((everyone, columns), lambda i: (0, i)),
            hbm, hbm,
        ],
        out_specs=(pl.BlockSpec((block, columns), lambda i: (0, i)), hbm, hbm),
        scratch_shapes=[pltpu.VMEM((padded, everyone), bf16), dma((2,))],
        compiler_params=pltpu.CompilerParams(vmem_limit_bytes=48 * 1024 * 1024),
        cost_estimate=pl.CostEstimate(
            flops=2 * everyone * padded * width, transcendentals=0,
            bytes_accessed=2 * everyone * width + 4 * block * width),
        name="weight",
    )(all_hidden.reshape(nodes * tokens, padded), all_grad, gg, gu)
    return gg, gu, grad_weight


def solution(mesh):
    nodes, local = mesh.shape["node"], mesh.shape["local"]
    devices = nodes * local

    def on_device(grad_out, gate_pre, up_pre, w_down):
        gather_bytes = devices * grad_out.size * 2
        sum_bytes = w_down.size * 4
        fits = local == 4 and nodes % 2 == 0 and grad_out.shape[0] % 16 == 0
        if fits and gather_bytes < sum_bytes and w_down.size <= 2 ** 24:
            return gathered(nodes, grad_out, gate_pre, up_pre, w_down)
        return summed(grad_out, gate_pre, up_pre, w_down)

    return jax.shard_map(
        on_device,
        mesh=mesh,
        in_specs=(
            P(("node", "local"), None),
            P("node", "local"),
            P("node", "local"),
            P("local", None),
        ),
        out_specs=(P("node", "local"), P("node", "local"), P(("local", "node"), None)),
        check_vma=False,
    )
```

```python
import functools

import jax
import jax.numpy as jnp
from jax import lax
from jax.experimental import pallas as pl
from jax.experimental.pallas import tpu as pltpu
from jax.sharding import PartitionSpec as P

MESH = pl.DeviceIdType.MESH
LANES = 128
STEP = 384


def factors(gate_pre, up_pre):
    gate = gate_pre.astype(jnp.float32)
    up = up_pre.astype(jnp.float32)
    sig = jax.nn.sigmoid(gate)
    return gate, up, sig, gate * sig


def summed(grad_out, gate_pre, up_pre, w_down):
    gate, up, sig, act = factors(gate_pre, up_pre)
    hidden = (act * up).astype(jnp.bfloat16)
    node_grad = lax.all_gather(grad_out, "local", axis=0, tiled=True)
    grad_hidden = jnp.einsum("td,fd->tf", node_grad, w_down, preferred_element_type=jnp.float32)
    grad_up = (grad_hidden * act).astype(jnp.bfloat16)
    grad_gate = (grad_hidden * up * sig * (1.0 + gate * (1.0 - sig))).astype(jnp.bfloat16)
    partial_value = jnp.einsum("tf,td->fd", hidden, node_grad, preferred_element_type=jnp.float32)
    grad_weight = lax.psum_scatter(partial_value, "node", scatter_dimension=0, tiled=True)
    return (grad_gate, grad_up, grad_weight)


def exchange(nodes, go_in, gate_in, up_in, w, all_grad, all_hidden, gg_out, gu_out,
             go, gate, up, gg, gu, wv, ng, hf, hs, xs, xr, ys, yr, xhs, xhr, yhs, yhr, zs, zr, ss, sr, hss, hsr, ws, ls):
    n, l = lax.axis_index("node"), lax.axis_index("local")
    levels = nodes // 2
    z, c = lax.div(n, 2), lax.rem(n, 2)
    y, x = lax.div(l, 2), lax.rem(l, 2)
    lx, ly, ld = y * 2 + 1 - x, (1 - y) * 2 + x, (1 - y) * 2 + 1 - x
    xn, yn, sib = (n, lx), (n, ly), (z * 2 + 1 - c, l)
    rows, width = go.shape
    half = width // 2
    tokens, hidden_units = gate.shape
    block = hidden_units // nodes
    padded = hs.shape[2]

    first = pltpu.make_async_copy(go_in, go, ls.at[7])
    first.start()
    loads = [pltpu.make_async_copy(gate_in, gate, ls.at[3]), pltpu.make_async_copy(up_in, up, ls.at[4])]
    for copy in loads:
        copy.start()

    starts = list(range(0, hidden_units, STEP))
    full = hidden_units // STEP

    def w_copy(i, size=STEP):
        at = pl.ds(i * STEP if isinstance(i, int) else pl.multiple_of(i * STEP, STEP), size)
        return pltpu.make_async_copy(w.at[at, :], wv.at[at, :], ws.at[i])

    for i, start in enumerate(starts):
        w_copy(i, min(STEP, hidden_units - start)).start()

    barrier = pltpu.get_barrier_semaphore()
    for peer in [xn, yn] + [(lax.rem(n + k, nodes), l) for k in range(1, nodes)]:
        pl.semaphore_signal(barrier, inc=1, device_id=peer, device_id_type=MESH)
    pl.semaphore_wait(barrier, nodes + 1)

    def slot(level, core, local, part=None):
        at = pl.ds(pl.multiple_of(((level * 2 + core) * 4 + local) * rows, rows), rows)
        if part is None:
            return all_grad.at[at, :]
        return all_grad.at[at, pl.ds(part * half, half)]

    def remote(source, target, sent, received, device):
        return pltpu.make_async_remote_copy(
            src_ref=source, dst_ref=target, send_sem=sent, recv_sem=received,
            device_id=device, device_id_type=MESH)

    def arrived(target, received):
        remote(target, target, hss.at[0], received, xn).wait_recv()

    start, sent = (lambda copy: copy.start()), (lambda copy: copy.wait_send())

    def along(level, source, side, act):
        can = z > 0 if side < 0 else z < levels - 1
        to = (n + 2 * side, l)

        @pl.when(can)
        def _():
            act(remote(source, slot(level, c, l), zs.at[(side + 1) // 2, level], zr.at[level], to))

    def across(level, source, act):
        target = slot(level, c, l)
        act(remote(source, target, xs.at[level], xr.at[level], xn))
        act(remote(source, target, ys.at[level], yr.at[level], yn))
        act(remote(source, target, ss.at[level, l], sr.at[level, l], sib))

    def from_x(level, act):
        part, whole = slot(level, c, lx, 0), slot(level, c, lx)
        act(remote(part, part, yhs.at[level], yhr.at[level], yn))
        act(remote(whole, whole, ss.at[level, lx], sr.at[level, lx], sib))

    def from_y(level, act):
        part, whole = slot(level, c, ly, 1), slot(level, c, ly)
        act(remote(part, part, xhs.at[level], xhr.at[level], xn))
        act(remote(whole, whole, ss.at[level, ly], sr.at[level, ly], sib))

    def from_d(level, act):
        whole = slot(level, c, ld)
        act(remote(whole, whole, ss.at[level, ld], sr.at[level, ld], sib))

    def each(distance, run):
        for side in (-1, 1):
            level = z + side * distance

            @pl.when((level >= 0) & (level < levels))
            def _():
                run(level, side)

    def z_event(level, side):
        arrived(slot(level, c, l), zr.at[level])
        source = slot(level, c, l)
        along(level, source, -side, start)
        across(level, source, start)

    def xy_event(level, side=0):
        arrived(slot(level, c, lx), xr.at[level])
        from_x(level, start)
        arrived(slot(level, c, ly), yr.at[level])
        from_y(level, start)

    def d_event(level, side=0):
        arrived(slot(level, c, ld, 0), yhr.at[level])
        arrived(slot(level, c, ld, 1), xhr.at[level])
        from_d(level, start)

    first.wait()
    for side in (-1, 1):
        along(z, go, side, start)
    across(z, go, start)
    own = pltpu.make_async_copy(go, slot(z, c, l), ls.at[0])
    own.start()

    for copy in loads:
        copy.wait()

    spread = hf.shape[1]
    last = hidden_units // LANES * LANES
    if spread > last:
        hf[:, last:] = jnp.zeros((tokens, spread - last), jnp.float32)

    @pl.loop(0, tokens // 16)
    def _(i):
        at = pl.ds(pl.multiple_of(i * 16, 16), 16)
        for first in range(0, hidden_units, 512):
            columns = slice(first, min(first + 512, hidden_units))
            g = gate[at, columns].astype(jnp.float32)
            hf[at, columns] = g * jax.nn.sigmoid(g) * up[at, columns].astype(jnp.float32)

    @pl.loop(0, tokens // 16)
    def _(i):
        at = pl.ds(pl.multiple_of(i * 16, 16), 16)
        for k in range(nodes):
            base = k * block // LANES * LANES
            shift = k * block - base
            window = padded + (LANES if shift else 0)
            values = hf[at, base:base + window]
            if shift:
                values = pltpu.roll(values, window - shift, 1)[:, :padded]
            hs[k, at, :] = values.astype(jnp.bfloat16)

    def hidden_copy(k):
        to = lax.rem(n + k, nodes)
        return remote(hs.at[to], all_hidden.at[n], hss.at[k], hsr.at[n], (to, l))

    own_hidden = pltpu.make_async_copy(hs.at[n], all_hidden.at[n], ls.at[1])
    own_hidden.start()

    def multiply(i, size=STEP):
        w_copy(i, size).wait()
        at = pl.ds(i * STEP if isinstance(i, int) else pl.multiple_of(i * STEP, STEP), size)
        grad = lax.dot_general(ng[...], wv[at, :], (((1,), (1,)), ((), ())),
                               preferred_element_type=jnp.float32)
        g, u = gate[:, at].astype(jnp.float32), up[:, at].astype(jnp.float32)
        sig = jax.nn.sigmoid(g)
        gu[:, at] = (grad * (g * sig)).astype(jnp.bfloat16)
        gg[:, at] = (grad * u * sig * (1.0 + g * (1.0 - sig))).astype(jnp.bfloat16)

    def multiply_some(part, parts):
        first, stop = full * part // parts, full * (part + 1) // parts

        @pl.loop(first, stop)
        def _(i):
            multiply(i)

    if levels > 1:
        each(1, z_event)
    xy_event(z)
    d_event(z)
    own.wait()
    node_rows = pl.ds(pl.multiple_of(n * tokens, tokens), tokens)
    load = pltpu.make_async_copy(all_grad.at[node_rows, :], ng, ls.at[2])
    load.start()
    load.wait()
    parts = 2 * levels - 1
    for distance in range(1, levels):
        multiply_some(2 * distance - 2, parts)
        if distance + 1 < levels:
            each(distance + 1, z_event)
        for k in range(1 + (distance - 1) * nodes // levels, 1 + distance * nodes // levels):
            hidden_copy(k).start()
        each(distance, xy_event)
        multiply_some(2 * distance - 1, parts)
        each(distance, d_event)
    for k in range(1 + (levels - 1) * nodes // levels, nodes):
        hidden_copy(k).start()
    multiply_some(parts - 1, parts)
    if hidden_units % STEP:
        multiply(full, hidden_units % STEP)

    stores = [pltpu.make_async_copy(gg, gg_out, ls.at[5]), pltpu.make_async_copy(gu, gu_out, ls.at[6])]
    for copy in stores:
        copy.start()

    @pl.loop(0, levels)
    def _(level):
        for local in range(4):
            arrived(slot(level, 1 - c, local), sr.at[level, local])

    for k in range(1, nodes):
        other = lax.rem(n + k, nodes)
        arrived(all_hidden.at[other], hsr.at[other])
        hidden_copy(k).wait_send()
    own_hidden.wait()
    for copy in stores:
        copy.wait()

    def z_sent(level, side):
        along(level, slot(level, c, l), -side, sent)

    for side in (-1, 1):
        along(z, go, side, sent)
    for distance in range(1, levels):
        each(distance, z_sent)

    @pl.loop(0, levels)
    def _(level):
        across(level, slot(level, c, l), sent)
        from_x(level, sent)
        from_y(level, sent)
        from_d(level, sent)


def weight(hidden, grads, gg, gu, out, gg_out, gu_out, turned, sems):
    copies = [pltpu.make_async_copy(gg, gg_out, sems.at[0]), pltpu.make_async_copy(gu, gu_out, sems.at[1])]
    i = pl.program_id(0)

    @pl.when(i == 0)
    def _():
        for copy in copies:
            copy.start()
        turned[...] = hidden[...].T

    rows = out.shape[0]
    out[...] = jnp.dot(turned[...], grads[...], preferred_element_type=jnp.float32)[:rows]

    @pl.when(i == pl.num_programs(0) - 1)
    def _():
        for copy in copies:
            copy.wait()


def gathered(nodes, grad_out, gate_pre, up_pre, w_down):
    tokens, hidden_units = gate_pre.shape
    rows, width = grad_out.shape
    levels = nodes // 2
    block = hidden_units // nodes
    padded = -(-block // LANES) * LANES
    spread = max(k * block // LANES * LANES + padded + LANES for k in range(nodes))
    everyone = nodes * 4 * rows
    chunks = -(-hidden_units // STEP)
    hbm = pl.BlockSpec(memory_space=pl.ANY)
    dma = pltpu.SemaphoreType.DMA
    bf16 = jnp.bfloat16
    all_grad, all_hidden, gg, gu = pl.pallas_call(
        functools.partial(exchange, nodes),
        out_shape=(
            jax.ShapeDtypeStruct((everyone, width), bf16),
            jax.ShapeDtypeStruct((nodes, tokens, padded), bf16),
            jax.ShapeDtypeStruct(gate_pre.shape, bf16),
            jax.ShapeDtypeStruct(gate_pre.shape, bf16),
        ),
        in_specs=[hbm] * 4,
        out_specs=(hbm,) * 4,
        scratch_shapes=[pltpu.VMEM(grad_out.shape, bf16)] + [pltpu.VMEM(gate_pre.shape, bf16)] * 4 + [
            pltpu.VMEM(w_down.shape, bf16),
            pltpu.VMEM((tokens, width), bf16),
            pltpu.VMEM((tokens, spread), jnp.float32),
            pltpu.VMEM((nodes, tokens, padded), bf16),
        ] + [dma((levels,))] * 8 + [
            dma((2, levels)), dma((levels,)),
            dma((levels, 4)), dma((levels, 4)),
            dma((nodes,)), dma((nodes,)),
            dma((chunks,)), dma((8,)),
        ],
        compiler_params=pltpu.CompilerParams(
            collective_id=0, has_side_effects=True, vmem_limit_bytes=56 * 1024 * 1024),
        cost_estimate=pl.CostEstimate(
            flops=2 * tokens * hidden_units * width, transcendentals=2 * tokens * hidden_units,
            bytes_accessed=2 * w_down.size),
        name="exchange",
    )(grad_out, gate_pre, up_pre, w_down)

    columns = 2048
    grad_weight, gg, gu = pl.pallas_call(
        weight,
        grid=(width // columns,),
        out_shape=(
            jax.ShapeDtypeStruct((block, width), jnp.float32),
            jax.ShapeDtypeStruct(gate_pre.shape, bf16),
            jax.ShapeDtypeStruct(gate_pre.shape, bf16),
        ),
        in_specs=[
            pl.BlockSpec((everyone // 4 // rows * tokens, padded), lambda i: (0, 0)),
            pl.BlockSpec((everyone, columns), lambda i: (0, i)),
            pl.BlockSpec(gate_pre.shape, lambda i: (0, 0)),
            pl.BlockSpec(gate_pre.shape, lambda i: (0, 0)),
        ],
        out_specs=(pl.BlockSpec((block, columns), lambda i: (0, i)), hbm, hbm),
        scratch_shapes=[pltpu.VMEM((padded, everyone), bf16), dma((2,))],
        compiler_params=pltpu.CompilerParams(vmem_limit_bytes=60 * 1024 * 1024),
        cost_estimate=pl.CostEstimate(
            flops=2 * everyone * padded * width, transcendentals=0,
            bytes_accessed=2 * everyone * width + 4 * block * width),
        name="weight",
    )(all_hidden.reshape(nodes * tokens, padded), all_grad, gg, gu)
    return gg, gu, grad_weight


def solution(mesh):
    nodes, local = mesh.shape["node"], mesh.shape["local"]
    devices = nodes * local

    def on_device(grad_out, gate_pre, up_pre, w_down):
        gather_bytes = devices * grad_out.size * 2
        sum_bytes = w_down.size * 4
        fits = local == 4 and nodes % 2 == 0 and grad_out.shape[0] % 16 == 0
        if fits and gather_bytes < sum_bytes and w_down.size <= 2 ** 24:
            return gathered(nodes, grad_out, gate_pre, up_pre, w_down)
        return summed(grad_out, gate_pre, up_pre, w_down)

    return jax.shard_map(
        on_device,
        mesh=mesh,
        in_specs=(
            P(("node", "local"), None),
            P("node", "local"),
            P("node", "local"),
            P("local", None),
        ),
        out_specs=(P("node", "local"), P("node", "local"), P(("local", "node"), None)),
        check_vma=False,
    )
```

```python
import functools

import jax
import jax.numpy as jnp
from jax import lax
from jax.experimental import pallas as pl
from jax.experimental.pallas import tpu as pltpu
from jax.sharding import PartitionSpec as P

MESH = pl.DeviceIdType.MESH
LANES = 128
STEP = 384


def factors(gate_pre, up_pre):
    gate = gate_pre.astype(jnp.float32)
    up = up_pre.astype(jnp.float32)
    sig = jax.nn.sigmoid(gate)
    return gate, up, sig, gate * sig


def summed(grad_out, gate_pre, up_pre, w_down):
    gate, up, sig, act = factors(gate_pre, up_pre)
    hidden = (act * up).astype(jnp.bfloat16)
    node_grad = lax.all_gather(grad_out, "local", axis=0, tiled=True)
    grad_hidden = jnp.einsum("td,fd->tf", node_grad, w_down, preferred_element_type=jnp.float32)
    grad_up = (grad_hidden * act).astype(jnp.bfloat16)
    grad_gate = (grad_hidden * up * sig * (1.0 + gate * (1.0 - sig))).astype(jnp.bfloat16)
    partial_value = jnp.einsum("tf,td->fd", hidden, node_grad, preferred_element_type=jnp.float32)
    grad_weight = lax.psum_scatter(partial_value, "node", scatter_dimension=0, tiled=True)
    return (grad_gate, grad_up, grad_weight)


def exchange(nodes, go_in, gate_in, up_in, w, all_grad, all_hidden, gg_out, gu_out,
             go, gate, up, gg, gu, wv, ng, hf, hs, xs, xr, ys, yr, xhs, xhr, yhs, yhr, zs, zr, ss, sr, hss, hsr, ws, ls):
    n, l = lax.axis_index("node"), lax.axis_index("local")
    levels = nodes // 2
    z, c = lax.div(n, 2), lax.rem(n, 2)
    y, x = lax.div(l, 2), lax.rem(l, 2)
    lx, ly, ld = y * 2 + 1 - x, (1 - y) * 2 + x, (1 - y) * 2 + 1 - x
    xn, yn, sib = (n, lx), (n, ly), (z * 2 + 1 - c, l)
    rows, width = go.shape
    half = width // 2
    tokens, hidden_units = gate.shape
    block = hidden_units // nodes
    padded = hs.shape[2]

    first = pltpu.make_async_copy(go_in, go, ls.at[7])
    first.start()
    loads = [pltpu.make_async_copy(gate_in, gate, ls.at[3]), pltpu.make_async_copy(up_in, up, ls.at[4])]
    for copy in loads:
        copy.start()

    starts = list(range(0, hidden_units, STEP))
    full = hidden_units // STEP

    def w_copy(i, size=STEP):
        at = pl.ds(i * STEP if isinstance(i, int) else pl.multiple_of(i * STEP, STEP), size)
        return pltpu.make_async_copy(w.at[at, :], wv.at[at, :], ws.at[i])

    for i, start in enumerate(starts):
        w_copy(i, min(STEP, hidden_units - start)).start()

    barrier = pltpu.get_barrier_semaphore()
    for peer in [xn, yn] + [(lax.rem(n + k, nodes), l) for k in range(1, nodes)]:
        pl.semaphore_signal(barrier, inc=1, device_id=peer, device_id_type=MESH)
    pl.semaphore_wait(barrier, nodes + 1)

    def slot(level, core, local, part=None):
        at = pl.ds(pl.multiple_of(((level * 2 + core) * 4 + local) * rows, rows), rows)
        if part is None:
            return all_grad.at[at, :]
        return all_grad.at[at, pl.ds(part * half, half)]

    def remote(source, target, sent, received, device):
        return pltpu.make_async_remote_copy(
            src_ref=source, dst_ref=target, send_sem=sent, recv_sem=received,
            device_id=device, device_id_type=MESH)

    def arrived(target, received):
        remote(target, target, hss.at[0], received, xn).wait_recv()

    start, sent = (lambda copy: copy.start()), (lambda copy: copy.wait_send())

    def along(level, source, side, act):
        can = z > 0 if side < 0 else z < levels - 1
        to = (n + 2 * side, l)

        @pl.when(can)
        def _():
            act(remote(source, slot(level, c, l), zs.at[(side + 1) // 2, level], zr.at[level], to))

    def across(level, source, act):
        target = slot(level, c, l)
        act(remote(source, target, xs.at[level], xr.at[level], xn))
        act(remote(source, target, ys.at[level], yr.at[level], yn))
        act(remote(source, target, ss.at[level, l], sr.at[level, l], sib))

    def from_x(level, act):
        part, whole = slot(level, c, lx, 0), slot(level, c, lx)
        act(remote(part, part, yhs.at[level], yhr.at[level], yn))
        act(remote(whole, whole, ss.at[level, lx], sr.at[level, lx], sib))

    def from_y(level, act):
        part, whole = slot(level, c, ly, 1), slot(level, c, ly)
        act(remote(part, part, xhs.at[level], xhr.at[level], xn))
        act(remote(whole, whole, ss.at[level, ly], sr.at[level, ly], sib))

    def from_d(level, act):
        whole = slot(level, c, ld)
        act(remote(whole, whole, ss.at[level, ld], sr.at[level, ld], sib))

    def each(distance, run):
        for side in (-1, 1):
            level = z + side * distance

            @pl.when((level >= 0) & (level < levels))
            def _():
                run(level, side)

    def z_event(level, side):
        arrived(slot(level, c, l), zr.at[level])
        source = slot(level, c, l)
        along(level, source, -side, start)
        across(level, source, start)

    def xy_event(level, side=0):
        arrived(slot(level, c, lx), xr.at[level])
        from_x(level, start)
        arrived(slot(level, c, ly), yr.at[level])
        from_y(level, start)

    def d_event(level, side=0):
        arrived(slot(level, c, ld, 0), yhr.at[level])
        arrived(slot(level, c, ld, 1), xhr.at[level])
        from_d(level, start)

    first.wait()
    for side in (-1, 1):
        along(z, go, side, start)
    across(z, go, start)
    own = pltpu.make_async_copy(go, slot(z, c, l), ls.at[0])
    own.start()

    for copy in loads:
        copy.wait()

    spread = hf.shape[1]
    last = hidden_units // LANES * LANES
    if spread > last:
        hf[:, last:] = jnp.zeros((tokens, spread - last), jnp.float32)

    @pl.loop(0, tokens // 16)
    def _(i):
        at = pl.ds(pl.multiple_of(i * 16, 16), 16)
        for first in range(0, hidden_units, 512):
            columns = slice(first, min(first + 512, hidden_units))
            g = gate[at, columns].astype(jnp.float32)
            hf[at, columns] = g * jax.nn.sigmoid(g) * up[at, columns].astype(jnp.float32)

    @pl.loop(0, tokens // 16)
    def _(i):
        at = pl.ds(pl.multiple_of(i * 16, 16), 16)
        for k in range(nodes):
            base = k * block // LANES * LANES
            shift = k * block - base
            window = padded + (LANES if shift else 0)
            values = hf[at, base:base + window]
            if shift:
                values = pltpu.roll(values, window - shift, 1)[:, :padded]
            hs[k, at, :] = values.astype(jnp.bfloat16)

    def hidden_copy(k):
        to = lax.rem(n + k, nodes)
        return remote(hs.at[to], all_hidden.at[n], hss.at[k], hsr.at[n], (to, l))

    own_hidden = pltpu.make_async_copy(hs.at[n], all_hidden.at[n], ls.at[1])
    own_hidden.start()

    def multiply(i, size=STEP):
        w_copy(i, size).wait()
        at = pl.ds(i * STEP if isinstance(i, int) else pl.multiple_of(i * STEP, STEP), size)
        grad = lax.dot_general(ng[...], wv[at, :], (((1,), (1,)), ((), ())),
                               preferred_element_type=jnp.float32)
        g, u = gate[:, at].astype(jnp.float32), up[:, at].astype(jnp.float32)
        sig = jax.nn.sigmoid(g)
        gu[:, at] = (grad * (g * sig)).astype(jnp.bfloat16)
        gg[:, at] = (grad * u * sig * (1.0 + g * (1.0 - sig))).astype(jnp.bfloat16)

    def multiply_some(part, parts):
        first, stop = full * part // parts, full * (part + 1) // parts

        @pl.loop(first, stop)
        def _(i):
            multiply(i)

    if levels > 1:
        each(1, z_event)
    xy_event(z)
    d_event(z)
    own.wait()
    node_rows = pl.ds(pl.multiple_of(n * tokens, tokens), tokens)
    load = pltpu.make_async_copy(all_grad.at[node_rows, :], ng, ls.at[2])
    load.start()
    load.wait()
    parts = 2 * levels - 1
    for distance in range(1, levels):
        multiply_some(2 * distance - 2, parts)
        if distance + 1 < levels:
            each(distance + 1, z_event)
        final = distance + 1 == levels
        for k in range(1 + (distance - 1) * nodes // levels, nodes if final else 1 + distance * nodes // levels):
            hidden_copy(k).start()
        if final:
            multiply_some(2 * distance - 1, parts)
        each(distance, xy_event)
        if final:
            multiply_some(parts - 1, parts)
            if hidden_units % STEP:
                multiply(full, hidden_units % STEP)
        else:
            multiply_some(2 * distance - 1, parts)
        each(distance, d_event)
    stores = [pltpu.make_async_copy(gg, gg_out, ls.at[5]), pltpu.make_async_copy(gu, gu_out, ls.at[6])]
    for copy in stores:
        copy.start()

    @pl.loop(0, levels)
    def _(level):
        for local in range(4):
            arrived(slot(level, 1 - c, local), sr.at[level, local])

    for k in range(1, nodes):
        other = lax.rem(n + k, nodes)
        arrived(all_hidden.at[other], hsr.at[other])
        hidden_copy(k).wait_send()
    own_hidden.wait()
    for copy in stores:
        copy.wait()

    def z_sent(level, side):
        along(level, slot(level, c, l), -side, sent)

    for side in (-1, 1):
        along(z, go, side, sent)
    for distance in range(1, levels):
        each(distance, z_sent)

    @pl.loop(0, levels)
    def _(level):
        across(level, slot(level, c, l), sent)
        from_x(level, sent)
        from_y(level, sent)
        from_d(level, sent)


def weight(hidden, grads, gg, gu, out, gg_out, gu_out, turned, sems):
    copies = [pltpu.make_async_copy(gg, gg_out, sems.at[0]), pltpu.make_async_copy(gu, gu_out, sems.at[1])]
    i = pl.program_id(0)

    @pl.when(i == 0)
    def _():
        for copy in copies:
            copy.start()
        turned[...] = hidden[...].T

    rows = out.shape[0]
    out[...] = jnp.dot(turned[...], grads[...], preferred_element_type=jnp.float32)[:rows]

    @pl.when(i == pl.num_programs(0) - 1)
    def _():
        for copy in copies:
            copy.wait()


def gathered(nodes, grad_out, gate_pre, up_pre, w_down):
    tokens, hidden_units = gate_pre.shape
    rows, width = grad_out.shape
    levels = nodes // 2
    block = hidden_units // nodes
    padded = -(-block // LANES) * LANES
    spread = max(k * block // LANES * LANES + padded + LANES for k in range(nodes))
    everyone = nodes * 4 * rows
    chunks = -(-hidden_units // STEP)
    hbm = pl.BlockSpec(memory_space=pl.ANY)
    dma = pltpu.SemaphoreType.DMA
    bf16 = jnp.bfloat16
    all_grad, all_hidden, gg, gu = pl.pallas_call(
        functools.partial(exchange, nodes),
        out_shape=(
            jax.ShapeDtypeStruct((everyone, width), bf16),
            jax.ShapeDtypeStruct((nodes, tokens, padded), bf16),
            jax.ShapeDtypeStruct(gate_pre.shape, bf16),
            jax.ShapeDtypeStruct(gate_pre.shape, bf16),
        ),
        in_specs=[hbm] * 4,
        out_specs=(hbm,) * 4,
        scratch_shapes=[pltpu.VMEM(grad_out.shape, bf16)] + [pltpu.VMEM(gate_pre.shape, bf16)] * 4 + [
            pltpu.VMEM(w_down.shape, bf16),
            pltpu.VMEM((tokens, width), bf16),
            pltpu.VMEM((tokens, spread), jnp.float32),
            pltpu.VMEM((nodes, tokens, padded), bf16),
        ] + [dma((levels,))] * 8 + [
            dma((2, levels)), dma((levels,)),
            dma((levels, 4)), dma((levels, 4)),
            dma((nodes,)), dma((nodes,)),
            dma((chunks,)), dma((8,)),
        ],
        compiler_params=pltpu.CompilerParams(
            collective_id=0, has_side_effects=True, vmem_limit_bytes=56 * 1024 * 1024),
        cost_estimate=pl.CostEstimate(
            flops=2 * tokens * hidden_units * width, transcendentals=2 * tokens * hidden_units,
            bytes_accessed=2 * w_down.size),
        name="exchange",
    )(grad_out, gate_pre, up_pre, w_down)

    columns = 2048
    grad_weight, gg, gu = pl.pallas_call(
        weight,
        grid=(width // columns,),
        out_shape=(
            jax.ShapeDtypeStruct((block, width), jnp.float32),
            jax.ShapeDtypeStruct(gate_pre.shape, bf16),
            jax.ShapeDtypeStruct(gate_pre.shape, bf16),
        ),
        in_specs=[
            pl.BlockSpec((everyone // 4 // rows * tokens, padded), lambda i: (0, 0)),
            pl.BlockSpec((everyone, columns), lambda i: (0, i)),
            pl.BlockSpec(gate_pre.shape, lambda i: (0, 0)),
            pl.BlockSpec(gate_pre.shape, lambda i: (0, 0)),
        ],
        out_specs=(pl.BlockSpec((block, columns), lambda i: (0, i)), hbm, hbm),
        scratch_shapes=[pltpu.VMEM((padded, everyone), bf16), dma((2,))],
        compiler_params=pltpu.CompilerParams(vmem_limit_bytes=60 * 1024 * 1024),
        cost_estimate=pl.CostEstimate(
            flops=2 * everyone * padded * width, transcendentals=0,
            bytes_accessed=2 * everyone * width + 4 * block * width),
        name="weight",
    )(all_hidden.reshape(nodes * tokens, padded), all_grad, gg, gu)
    return gg, gu, grad_weight


def solution(mesh):
    nodes, local = mesh.shape["node"], mesh.shape["local"]
    devices = nodes * local

    def on_device(grad_out, gate_pre, up_pre, w_down):
        gather_bytes = devices * grad_out.size * 2
        sum_bytes = w_down.size * 4
        fits = local == 4 and nodes % 2 == 0 and nodes > 2 and grad_out.shape[0] % 16 == 0
        if fits and gather_bytes < sum_bytes and w_down.size <= 2 ** 24:
            return gathered(nodes, grad_out, gate_pre, up_pre, w_down)
        return summed(grad_out, gate_pre, up_pre, w_down)

    return jax.shard_map(
        on_device,
        mesh=mesh,
        in_specs=(
            P(("node", "local"), None),
            P("node", "local"),
            P("node", "local"),
            P("local", None),
        ),
        out_specs=(P("node", "local"), P("node", "local"), P(("local", "node"), None)),
        check_vma=False,
    )
```
